32 devices in a mesh: grp: 2 (over x), tm: 16 (over z, y, core).
Axes of the slice: x: 2, y: 2, z: 4, core: 2. Of those that a mesh axis runs over, the one named last changes fastest.
Arguments:
- series: bfloat16 [3072, 49152], P('tm', 'grp'), parts along dimension 1, may hold values from -6 to 6
- filter_taps: bfloat16 [201], replicated, may hold values from -0.4375 to 0.4375
- test_matrix: bfloat16 [24576, 128], replicated, may hold values from -0.0390625 to 0.0390625
Outputs:
- patterns: float32 [49152, 128], P(('grp', 'tm')), parts along dimension 0
- factor: float32 [256, 128], P('grp'), parts along dimension 0
The draws below stay inside these ranges and needn't reach their ends.
There are 2 independent parts, one for each index of `grp`. The reference program is written for one: setup_inputs(seed, part) draws one part's arguments, and reference() takes and returns one part's arrays. A program takes and returns all parts, laid end to end along the dimension named above; an argument that names none is the same for every part. Nothing has to cross between parts.
All inputs are finite; a program needn't handle non-finite values.
Results may differ from the reference program's by a relative error of at most 0.0006.
The reference program's roundings to bfloat16 on the way (of `filtered` and `sketch`) count: a program that leaves them out, or rounds other values in their place, can miss the bound.
Values may be sent and summed in bfloat16 or wider, within the bound.
A program may use at most 128 MiB of HBM per device.

```python
import jax
import jax.numpy as jnp
from jax import lax

DAYS_DEV = 192
COLS = 24576
RANK = 128
TAPS = 201
HALF = 100
TIME = 3072


def block_scale(rng, dims, shards, low, largest):
    def one(position, blocks):
        steps = jax.random.uniform(jax.random.fold_in(jax.random.fold_in(rng, 6), position), (blocks,), jnp.float32, low / len(shards), largest / len(shards))
        return jnp.repeat(jnp.exp(steps), dims[position] // blocks).reshape((-1,) + (1,) * (len(dims) - position - 1))

    gain = one(*shards[0])
    for cut in shards[1:]:
        gain = gain * one(*cut)
    return gain


def gaussian(key, dims, spread, limit, cuts=(), kind=jnp.bfloat16):
    drawn = spread * jax.random.normal(key, dims, jnp.float32)
    if cuts:
        drawn = drawn * block_scale(key, dims, cuts, -0.22, 0.18)
    return jnp.clip(drawn, -limit, limit).astype(kind)


def setup_inputs(seed: int = 0, part: int = 0) -> dict:
    streams_of = jax.random.split(jax.random.key(seed), 4)
    own_keys = jax.random.split(jax.random.fold_in(streams_of[3], part), 4)
    return {
        "series": gaussian(own_keys[0], (TIME, COLS), 1.0, 6.0, ((0, 16),)),
        "filter_taps": gaussian(streams_of[1], (TAPS,), TAPS ** -0.5, 0.4375),
        "test_matrix": gaussian(streams_of[2], (COLS, RANK), COLS ** -0.5, 0.0390625),
    }


def toeplitz_rows(filter_taps, day_count):
    width = filter_taps.shape[0]
    row_len = width + day_count
    padded_taps = jnp.concatenate([filter_taps, jnp.zeros((day_count,), filter_taps.dtype)])
    flat = jnp.tile(padded_taps, day_count)[:day_count * (row_len - 1)]
    return flat.reshape(day_count, row_len - 1)

def reference(series, filter_taps, test_matrix):
    toeplitz = toeplitz_rows(filter_taps, DAYS_DEV)
    padded = jnp.pad(series, ((HALF, HALF), (0, 0)))
    starts = jnp.arange(TIME // DAYS_DEV, dtype=jnp.int32) * DAYS_DEV

    def one_block(first_row):
        window = lax.dynamic_slice_in_dim(padded, first_row, DAYS_DEV + 2 * HALF, 0)
        return jnp.dot(toeplitz.astype(jnp.float32), window.astype(jnp.float32), preferred_element_type=jnp.float32).astype(jnp.bfloat16)
    filtered = lax.map(one_block, starts).reshape(TIME, COLS)
    sketch = jnp.dot(filtered.astype(jnp.float32), test_matrix.astype(jnp.float32), preferred_element_type=jnp.float32).astype(jnp.bfloat16)
    gram_sum = jnp.einsum('tr,ts->rs', sketch.astype(jnp.float32), sketch.astype(jnp.float32), preferred_element_type=jnp.float32)
    lower_factor = jnp.linalg.cholesky(gram_sum)
    cross_sums = jnp.einsum('tc,tr->cr', filtered.astype(jnp.float32), sketch.astype(jnp.float32), preferred_element_type=jnp.float32)
    patterns = lax.linalg.triangular_solve(lower_factor, cross_sums, left_side=False, lower=True, transpose_a=True)
    factor = lower_factor.T * float(TIME) ** (-0.5)
    return (patterns, factor)
```

```python
import functools

import jax
import jax.numpy as jnp
from jax import lax
from jax.experimental import pallas as pl
from jax.experimental.pallas import tpu as pltpu
from jax.sharding import Mesh, PartitionSpec as P

MESH = pl.DeviceIdType.MESH
TEAM = 4
BLOCK = 256


def banded_rows(filter_taps, rows, width, lead):
    taps = filter_taps.shape[0]
    line = jnp.concatenate(
        [jnp.zeros((lead,), filter_taps.dtype), filter_taps, jnp.zeros((width + 1 - lead - taps,), filter_taps.dtype)]
    )
    return jnp.tile(line, rows)[: rows * width].reshape(rows, width)


def team_kernel(
    cut, teams, pad,
    series, band, omega, cross, gram,
    days, filt, om, acc, got, sk,
    local_sem, om_sem, send_sem, recv_sem, hsend, hrecv, ssend, srecv, gsend, grecv,
):
    z, q = lax.axis_index("z"), lax.axis_index("q")
    own = series.shape[0]
    width = filt.shape[1]
    per = width // teams
    span = own * TEAM
    chunks = width // cut
    subs = per // cut
    up, down = lax.rem(z + 1, teams), lax.rem(z + teams - 1, teams)

    barrier = pltpu.get_barrier_semaphore()
    for d in range(1, TEAM):
        pl.semaphore_signal(barrier, inc=1, device_id={"q": lax.rem(q + d, TEAM)}, device_id_type=MESH)
    for other in (up, down):
        pl.semaphore_signal(barrier, inc=1, device_id={"z": other}, device_id_type=MESH)

    def source(k, member):
        start = ((k // subs) * TEAM + member) * per + (k % subs) * cut
        return series.at[:, pl.ds(pl.multiple_of(start, 128), cut)]

    def cols(k):
        return pl.ds(pl.multiple_of(k * cut, 128), cut)

    mine = pl.ds(pl.multiple_of(pad + q * own, 16), own)
    share = pl.ds(pl.multiple_of(q * own, 16), own)

    def local(k):
        return pltpu.make_async_copy(source(k, q), days.at[mine, cols(k)], local_sem.at[k])

    def omega_rows(b):
        rows = pl.ds(pl.multiple_of((b * TEAM + q) * per, 128), per)
        return pltpu.make_async_copy(omega.at[rows, :], om.at[pl.ds(b * per, per), :], om_sem.at[b])

    def give(k, d):
        peer = lax.rem(q + d, TEAM)
        return pltpu.make_async_remote_copy(
            src_ref=source(k, peer), dst_ref=days.at[mine, cols(k)],
            send_sem=send_sem.at[k, d - 1], recv_sem=recv_sem.at[k, d - 1],
            device_id={"q": peer}, device_id_type=MESH,
        )

    def take(k, d):
        origin = lax.rem(q + TEAM - d, TEAM)
        rows = pl.ds(pl.multiple_of(pad + origin * own, 16), own)
        return pltpu.make_async_remote_copy(
            src_ref=days.at[rows, cols(k)], dst_ref=days.at[rows, cols(k)],
            send_sem=send_sem.at[k, d - 1], recv_sem=recv_sem.at[k, d - 1],
            device_id={"q": origin}, device_id_type=MESH,
        )

    def halo_up(k):
        return pltpu.make_async_remote_copy(
            src_ref=days.at[pl.ds(span, pad), cols(k)], dst_ref=days.at[pl.ds(0, pad), cols(k)],
            send_sem=hsend.at[k, 0], recv_sem=hrecv.at[k, 0],
            device_id={"z": up}, device_id_type=MESH,
        )

    def halo_down(k):
        return pltpu.make_async_remote_copy(
            src_ref=days.at[pl.ds(pad, pad), cols(k)], dst_ref=days.at[pl.ds(pad + span, pad), cols(k)],
            send_sem=hsend.at[k, 1], recv_sem=hrecv.at[k, 1],
            device_id={"z": down}, device_id_type=MESH,
        )

    for b in range(teams):
        omega_rows(b).start()
    for k in range(chunks):
        local(k).start()
    pl.semaphore_wait(barrier, TEAM + 1)

    def give_all(k):
        for d in (2, 1, 3):
            give(k, d).start()

    ahead = 2
    for k in range(ahead):
        give_all(k)

    @pl.when(z == 0)
    def _():
        days[:pad, :] = jnp.zeros((pad, width), days.dtype)

    @pl.when(z == teams - 1)
    def _():
        days[pad + span :, :] = jnp.zeros((pad, width), days.dtype)

    acc[...] = jnp.zeros_like(acc)
    for b in range(teams):
        omega_rows(b).wait()

    reach = band.shape[1]

    def step(k, carry):
        @pl.when(k < chunks)
        def _():
            local(k).wait()
            for d in range(1, TEAM):
                take(k, d).wait_recv()

            @pl.when(z < teams - 1)
            def _():
                halo_up(k).start()

            @pl.when(z > 0)
            def _():
                halo_down(k).start()

        @pl.when(k + ahead < chunks)
        def _():
            give_all(k + ahead)

        @pl.when(k >= 1)
        def _():
            p = k - 1

            @pl.when(z > 0)
            def _():
                halo_up(p).wait_recv()

            @pl.when(z < teams - 1)
            def _():
                halo_down(p).wait_recv()

            weights = om[pl.ds(pl.multiple_of(p * cut, 128), cut), :]
            for r in range(span // BLOCK):
                part = jnp.dot(
                    band[...], days[r * BLOCK : r * BLOCK + reach, cols(p)], preferred_element_type=jnp.float32
                ).astype(filt.dtype)
                filt[r * BLOCK : (r + 1) * BLOCK, cols(p)] = part
                acc[r * BLOCK : (r + 1) * BLOCK, :] += jnp.dot(part, weights, preferred_element_type=jnp.float32)

        return carry

    lax.fori_loop(0, chunks + 1, step, 0)

    def part_copy(d):
        peer = lax.rem(q + d, TEAM)
        rows = pl.ds(pl.multiple_of(peer * own, 16), own)
        return pltpu.make_async_remote_copy(
            src_ref=acc.at[rows, :], dst_ref=got.at[d - 1],
            send_sem=ssend.at[d - 1], recv_sem=srecv.at[d - 1],
            device_id={"q": peer}, device_id_type=MESH,
        )

    def done_copy(d):
        return pltpu.make_async_remote_copy(
            src_ref=sk.at[share, :], dst_ref=sk.at[share, :],
            send_sem=gsend.at[d - 1], recv_sem=grecv.at[d - 1],
            device_id={"q": lax.rem(q + d, TEAM)}, device_id_type=MESH,
        )

    def done_take(d):
        origin = lax.rem(q + TEAM - d, TEAM)
        rows = pl.ds(pl.multiple_of(origin * own, 16), own)
        return pltpu.make_async_remote_copy(
            src_ref=sk.at[rows, :], dst_ref=sk.at[rows, :],
            send_sem=gsend.at[d - 1], recv_sem=grecv.at[d - 1],
            device_id={"q": origin}, device_id_type=MESH,
        )

    for d in (2, 1, 3):
        part_copy(d).start()
    for d in range(1, TEAM):
        part_copy(d).wait_recv()
    total = acc[share, :] + got[0] + got[1] + got[2]
    sk[share, :] = total.astype(sk.dtype)
    for d in (2, 1, 3):
        done_copy(d).start()
    for d in range(1, TEAM):
        done_take(d).wait_recv()

    sketch = sk[...]
    turned = sketch.T
    gram[...] = jnp.dot(turned, sketch, preferred_element_type=jnp.float32)

    def product(k, carry):
        cross[:, cols(k)] = jnp.dot(turned, filt[:, cols(k)], preferred_element_type=jnp.float32)
        return carry

    lax.fori_loop(0, chunks, product, 0)

    def drain(k, carry):
        for d in range(1, TEAM):
            give(k, d).wait_send()

        @pl.when(z < teams - 1)
        def _():
            halo_up(k).wait_send()

        @pl.when(z > 0)
        def _():
            halo_down(k).wait_send()

        return carry

    lax.fori_loop(0, chunks, drain, 0)
    for d in range(1, TEAM):
        part_copy(d).wait_send()
        done_copy(d).wait_send()


def on_device(teams, series, filter_taps, test_matrix):
    own, columns = series.shape
    rank = test_matrix.shape[1]
    half_width = (filter_taps.shape[0] - 1) // 2
    pad = -(-half_width // 16) * 16
    span = own * TEAM
    width = columns // TEAM
    per = width // teams
    cut = per // 2 if per % 256 == 0 and per > 512 else per
    chunks = width // cut
    band = banded_rows(filter_taps, BLOCK, BLOCK + 2 * pad, pad - half_width)
    vmem = pl.BlockSpec(memory_space=pltpu.VMEM)
    hbm = pl.BlockSpec(memory_space=pl.ANY)
    dma = pltpu.SemaphoreType.DMA
    flops = 2 * span * width * (BLOCK + 2 * pad + 2 * rank)
    cross, gram = pl.pallas_call(
        functools.partial(team_kernel, cut, teams, pad),
        out_shape=(
            jax.ShapeDtypeStruct((rank, width), jnp.float32),
            jax.ShapeDtypeStruct((rank, rank), jnp.float32),
        ),
        in_specs=[hbm, vmem, hbm],
        out_specs=(vmem, vmem),
        scratch_shapes=[
            pltpu.VMEM((span + 2 * pad, width), jnp.bfloat16),
            pltpu.VMEM((span, width), jnp.bfloat16),
            pltpu.VMEM((width, rank), jnp.bfloat16),
            pltpu.VMEM((span, rank), jnp.float32),
            pltpu.VMEM((TEAM - 1, own, rank), jnp.float32),
            pltpu.VMEM((span, rank), jnp.bfloat16),
            dma((chunks,)),
            dma((teams,)),
            dma((chunks, TEAM - 1)),
            dma((chunks, TEAM - 1)),
            dma((chunks, 2)),
            dma((chunks, 2)),
            dma((TEAM - 1,)),
            dma((TEAM - 1,)),
            dma((TEAM - 1,)),
            dma((TEAM - 1,)),
        ],
        compiler_params=pltpu.CompilerParams(
            collective_id=0, has_side_effects=True, vmem_limit_bytes=56 * 1024 * 1024
        ),
        cost_estimate=pl.CostEstimate(flops=flops, bytes_accessed=2 * own * columns * 3, transcendentals=0),
    )(series, band, test_matrix)
    gram_sum = lax.psum(gram, "z")
    cross_sums = lax.psum_scatter(cross.reshape(rank, teams, per).swapaxes(0, 1), "z", scatter_dimension=0, tiled=False)
    lower_factor = jnp.linalg.cholesky(gram_sum)
    patterns = lax.linalg.triangular_solve(
        lower_factor, cross_sums.T, left_side=False, lower=True, transpose_a=True
    )
    total_days = span * teams
    factor = lower_factor.T * float(total_days) ** (-0.5)
    return (patterns, factor)


def solution(mesh):
    groups, members = mesh.devices.shape
    teams = members // TEAM
    split = Mesh(mesh.devices.reshape(groups, teams, TEAM), ("grp", "z", "q"))
    placed = (P(("z", "q"), "grp"), P(), P())
    return jax.shard_map(
        functools.partial(on_device, teams),
        mesh=split,
        in_specs=placed,
        out_specs=(P(("grp", "z", "q"), None), P("grp", None)),
        check_vma=False,
    )
```

```python
import functools

import jax
import jax.numpy as jnp
from jax import lax
from jax.experimental import pallas as pl
from jax.experimental.pallas import tpu as pltpu
from jax.sharding import Mesh, PartitionSpec as P

MESH = pl.DeviceIdType.MESH
TEAM = 4
BLOCK = 256


def banded_rows(filter_taps, rows, width, lead):
    taps = filter_taps.shape[0]
    line = jnp.concatenate(
        [jnp.zeros((lead,), filter_taps.dtype), filter_taps, jnp.zeros((width + 1 - lead - taps,), filter_taps.dtype)]
    )
    return jnp.tile(line, rows)[: rows * width].reshape(rows, width)


def team_kernel(
    cut, teams, pad,
    series, band, omega, patterns, factor,
    days, filt, om, acc, got, sk, grams, tri, cross, landed,
    local_sem, om_sem, send_sem, recv_sem, hsend, hrecv, ssend, srecv, gsend, grecv, msend, mrecv, rsend, rrecv,
):
    z, q = lax.axis_index("z"), lax.axis_index("q")
    own = series.shape[0]
    width = filt.shape[1]
    per = width // teams
    span = own * TEAM
    chunks = width // cut
    subs = per // cut
    up, down = lax.rem(z + 1, teams), lax.rem(z + teams - 1, teams)

    barrier = pltpu.get_barrier_semaphore()
    for d in range(1, TEAM):
        pl.semaphore_signal(barrier, inc=1, device_id={"q": lax.rem(q + d, TEAM)}, device_id_type=MESH)
    for d in range(1, teams):
        pl.semaphore_signal(barrier, inc=1, device_id={"z": lax.rem(z + d, teams)}, device_id_type=MESH)

    def source(k, member):
        start = ((k // subs) * TEAM + member) * per + (k % subs) * cut
        return series.at[:, pl.ds(pl.multiple_of(start, 128), cut)]

    def cols(k):
        return pl.ds(pl.multiple_of(k * cut, 128), cut)

    mine = pl.ds(pl.multiple_of(pad + q * own, 16), own)
    share = pl.ds(pl.multiple_of(q * own, 16), own)

    def local(k):
        return pltpu.make_async_copy(source(k, q), days.at[mine, cols(k)], local_sem.at[k])

    def omega_rows(b):
        rows = pl.ds(pl.multiple_of((b * TEAM + q) * per, 128), per)
        return pltpu.make_async_copy(omega.at[rows, :], om.at[pl.ds(b * per, per), :], om_sem.at[b])

    def give(k, d):
        peer = lax.rem(q + d, TEAM)
        return pltpu.make_async_remote_copy(
            src_ref=source(k, peer), dst_ref=days.at[mine, cols(k)],
            send_sem=send_sem.at[k, d - 1], recv_sem=recv_sem.at[k, d - 1],
            device_id={"q": peer}, device_id_type=MESH,
        )

    def take(k, d):
        origin = lax.rem(q + TEAM - d, TEAM)
        rows = pl.ds(pl.multiple_of(pad + origin * own, 16), own)
        return pltpu.make_async_remote_copy(
            src_ref=days.at[rows, cols(k)], dst_ref=days.at[rows, cols(k)],
            send_sem=send_sem.at[k, d - 1], recv_sem=recv_sem.at[k, d - 1],
            device_id={"q": origin}, device_id_type=MESH,
        )

    def halo_up(k):
        return pltpu.make_async_remote_copy(
            src_ref=days.at[pl.ds(span, pad), cols(k)], dst_ref=days.at[pl.ds(0, pad), cols(k)],
            send_sem=hsend.at[k, 0], recv_sem=hrecv.at[k, 0],
            device_id={"z": up}, device_id_type=MESH,
        )

    def halo_down(k):
        return pltpu.make_async_remote_copy(
            src_ref=days.at[pl.ds(pad, pad), cols(k)], dst_ref=days.at[pl.ds(pad + span, pad), cols(k)],
            send_sem=hsend.at[k, 1], recv_sem=hrecv.at[k, 1],
            device_id={"z": down}, device_id_type=MESH,
        )

    for b in range(teams):
        omega_rows(b).start()
    for k in range(chunks):
        local(k).start()
    pl.semaphore_wait(barrier, TEAM + teams - 2)

    def give_all(k):
        for d in (2, 1, 3):
            give(k, d).start()

    ahead = 2
    for k in range(ahead):
        give_all(k)

    @pl.when(z == 0)
    def _():
        days[:pad, :] = jnp.zeros((pad, width), days.dtype)

    @pl.when(z == teams - 1)
    def _():
        days[pad + span :, :] = jnp.zeros((pad, width), days.dtype)

    acc[...] = jnp.zeros_like(acc)
    for b in range(teams):
        omega_rows(b).wait()

    reach = band.shape[1]

    def step(k, carry):
        @pl.when(k < chunks)
        def _():
            local(k).wait()
            for d in range(1, TEAM):
                take(k, d).wait_recv()

            @pl.when(z < teams - 1)
            def _():
                halo_up(k).start()

            @pl.when(z > 0)
            def _():
                halo_down(k).start()

        @pl.when(k + ahead < chunks)
        def _():
            give_all(k + ahead)

        @pl.when(k >= 1)
        def _():
            p = k - 1

            @pl.when(z > 0)
            def _():
                halo_up(p).wait_recv()

            @pl.when(z < teams - 1)
            def _():
                halo_down(p).wait_recv()

            weights = om[pl.ds(pl.multiple_of(p * cut, 128), cut), :]
            for r in range(span // BLOCK):
                part = jnp.dot(
                    band[...], days[r * BLOCK : r * BLOCK + reach, cols(p)], preferred_element_type=jnp.float32
                ).astype(filt.dtype)
                filt[r * BLOCK : (r + 1) * BLOCK, cols(p)] = part
                acc[r * BLOCK : (r + 1) * BLOCK, :] += jnp.dot(part, weights, preferred_element_type=jnp.float32)

        return carry

    lax.fori_loop(0, chunks + 1, step, 0)

    def part_copy(d):
        peer = lax.rem(q + d, TEAM)
        rows = pl.ds(pl.multiple_of(peer * own, 16), own)
        return pltpu.make_async_remote_copy(
            src_ref=acc.at[rows, :], dst_ref=got.at[d - 1],
            send_sem=ssend.at[d - 1], recv_sem=srecv.at[d - 1],
            device_id={"q": peer}, device_id_type=MESH,
        )

    def done_copy(d):
        return pltpu.make_async_remote_copy(
            src_ref=sk.at[share, :], dst_ref=sk.at[share, :],
            send_sem=gsend.at[d - 1], recv_sem=grecv.at[d - 1],
            device_id={"q": lax.rem(q + d, TEAM)}, device_id_type=MESH,
        )

    def done_take(d):
        origin = lax.rem(q + TEAM - d, TEAM)
        rows = pl.ds(pl.multiple_of(origin * own, 16), own)
        return pltpu.make_async_remote_copy(
            src_ref=sk.at[rows, :], dst_ref=sk.at[rows, :],
            send_sem=gsend.at[d - 1], recv_sem=grecv.at[d - 1],
            device_id={"q": origin}, device_id_type=MESH,
        )

    for d in (2, 1, 3):
        part_copy(d).start()
    for d in range(1, TEAM):
        part_copy(d).wait_recv()
    total = acc[share, :] + got[0] + got[1] + got[2]
    sk[share, :] = total.astype(sk.dtype)
    for d in (2, 1, 3):
        done_copy(d).start()
    for d in range(1, TEAM):
        done_take(d).wait_recv()

    sketch = sk[...]
    turned = sketch.T
    rank = sketch.shape[1]
    grams[0] = jnp.dot(turned, sketch, preferred_element_type=jnp.float32)

    def gram_copy(d):
        return pltpu.make_async_remote_copy(
            src_ref=grams.at[0], dst_ref=grams.at[d],
            send_sem=msend.at[d - 1], recv_sem=mrecv.at[d - 1],
            device_id={"z": lax.rem(z + d, teams)}, device_id_type=MESH,
        )

    for d in range(1, teams):
        gram_copy(d).start()

    def sum_right(c):
        return pltpu.make_async_remote_copy(
            src_ref=cross.at[c], dst_ref=landed.at[c],
            send_sem=rsend.at[c], recv_sem=rrecv.at[c],
            device_id={"z": up}, device_id_type=MESH,
        )

    def sum_left(c):
        slot = jnp.where(c == down, teams, c)
        return pltpu.make_async_remote_copy(
            src_ref=cross.at[c], dst_ref=landed.at[slot],
            send_sem=rsend.at[c], recv_sem=rrecv.at[slot],
            device_id={"z": down}, device_id_type=MESH,
        )

    def arrived(slot):
        return pltpu.make_async_remote_copy(
            src_ref=landed.at[slot], dst_ref=landed.at[slot],
            send_sem=rsend.at[0], recv_sem=rrecv.at[slot],
            device_id={"z": up}, device_id_type=MESH,
        )

    order = []
    for i in range((teams + 1) // 2):
        order += [teams - 1 - i] + ([i] if i != teams - 1 - i else [])
    for c in order:
        for s in range(subs):
            k = c * subs + s
            cross[c, :, s * cut : (s + 1) * cut] = jnp.dot(
                turned, filt[:, k * cut : (k + 1) * cut], preferred_element_type=jnp.float32
            )
        if c > 0:
            @pl.when(z == 0)
            def _():
                sum_right(c).start()
        if c < teams - 1:
            @pl.when(z == teams - 1)
            def _():
                sum_left(c).start()

    for d in range(1, teams):
        gram_copy(d).wait_recv()
    whole = grams[0]
    for d in range(1, teams):
        whole = whole + grams[d]
    row = lax.broadcasted_iota(jnp.int32, (rank, rank), 0)
    col = lax.broadcasted_iota(jnp.int32, (rank, rank), 1)
    tri[:, :rank] = whole
    tri[:, rank:] = jnp.where(row == col, 1.0, 0.0).astype(jnp.float32)
    lane = lax.broadcasted_iota(jnp.int32, (1, rank), 1)
    eye = row == col
    below = lax.broadcasted_iota(jnp.int32, (rank, 1), 0)

    def eliminate(j, carry):
        line = tri[pl.ds(j, 1), :]
        pivot = jnp.sum(jnp.where(lane == j, line[:, :rank], 0.0), axis=1, keepdims=True)
        line = line * (1.0 / jnp.sqrt(pivot))
        mult = jnp.sum(jnp.where(eye, line[:, :rank], 0.0), axis=1, keepdims=True)
        tri[...] = tri[...] - jnp.where(below > j, mult, 0.0) * line
        tri[pl.ds(j, 1), :] = line
        return carry

    piece = rank // teams
    for i in range(teams):
        lax.fori_loop(i * piece, (i + 1) * piece, eliminate, 0)
        if 0 < teams - 1 - i:
            c = teams - 1 - i
            @pl.when((z > 0) & (z < c))
            def _():
                arrived(c).wait_recv()
                cross[c] = cross[c] + landed[c]
                sum_right(c).start()
        if i < teams - 1:
            @pl.when((z < teams - 1) & (z > i))
            def _():
                arrived(i).wait_recv()
                cross[i] = cross[i] + landed[i]
                sum_left(i).start()

    upper = jnp.where(row <= col, tri[:, :rank], 0.0)
    factor[...] = upper * float(span * teams) ** (-0.5)
    inverse = jnp.where(row >= col, tri[:, rank:], 0.0)

    @pl.when(z > 0)
    def _():
        arrived(z).wait_recv()
        cross[z] = cross[z] + landed[z]

    @pl.when(z < teams - 1)
    def _():
        arrived(teams).wait_recv()
        cross[z] = cross[z] + landed[teams]

    for s in range(subs):
        solved = jnp.dot(
            inverse, cross[z, :, s * cut : (s + 1) * cut],
            preferred_element_type=jnp.float32, precision=lax.Precision.HIGHEST,
        )
        patterns[s * cut : (s + 1) * cut, :] = solved.T

    def drain(k, carry):
        for d in range(1, TEAM):
            give(k, d).wait_send()

        @pl.when(z < teams - 1)
        def _():
            halo_up(k).wait_send()

        @pl.when(z > 0)
        def _():
            halo_down(k).wait_send()

        return carry

    lax.fori_loop(0, chunks, drain, 0)
    for d in range(1, TEAM):
        part_copy(d).wait_send()
        done_copy(d).wait_send()
    for d in range(1, teams):
        gram_copy(d).wait_send()
    for c in range(teams):
        @pl.when(c != z)
        def _():
            sum_right(c).wait_send()


def on_device(teams, series, filter_taps, test_matrix):
    own, columns = series.shape
    rank = test_matrix.shape[1]
    half_width = (filter_taps.shape[0] - 1) // 2
    pad = -(-half_width // 16) * 16
    span = own * TEAM
    width = columns // TEAM
    per = width // teams
    cut = per // 2 if per % 256 == 0 and per > 512 else per
    chunks = width // cut
    band = banded_rows(filter_taps, BLOCK, BLOCK + 2 * pad, pad - half_width)
    vmem = pl.BlockSpec(memory_space=pltpu.VMEM)
    hbm = pl.BlockSpec(memory_space=pl.ANY)
    dma = pltpu.SemaphoreType.DMA
    flops = 2 * span * width * (BLOCK + 2 * pad + 2 * rank)
    return pl.pallas_call(
        functools.partial(team_kernel, cut, teams, pad),
        out_shape=(
            jax.ShapeDtypeStruct((per, rank), jnp.float32),
            jax.ShapeDtypeStruct((rank, rank), jnp.float32),
        ),
        in_specs=[hbm, vmem, hbm],
        out_specs=(vmem, vmem),
        scratch_shapes=[
            pltpu.VMEM((span + 2 * pad, width), jnp.bfloat16),
            pltpu.VMEM((span, width), jnp.bfloat16),
            pltpu.VMEM((width, rank), jnp.bfloat16),
            pltpu.VMEM((span, rank), jnp.float32),
            pltpu.VMEM((TEAM - 1, own, rank), jnp.float32),
            pltpu.VMEM((span, rank), jnp.bfloat16),
            pltpu.VMEM((teams, rank, rank), jnp.float32),
            pltpu.VMEM((rank, 2 * rank), jnp.float32),
            pltpu.VMEM((teams, rank, per), jnp.float32),
            pltpu.VMEM((teams + 1, rank, per), jnp.float32),
            dma((chunks,)),
            dma((teams,)),
            dma((chunks, TEAM - 1)),
            dma((chunks, TEAM - 1)),
            dma((chunks, 2)),
            dma((chunks, 2)),
            dma((TEAM - 1,)),
            dma((TEAM - 1,)),
            dma((TEAM - 1,)),
            dma((TEAM - 1,)),
            dma((teams - 1,)),
            dma((teams - 1,)),
            dma((teams,)),
            dma((teams + 1,)),
        ],
        compiler_params=pltpu.CompilerParams(
            collective_id=0, has_side_effects=True, vmem_limit_bytes=56 * 1024 * 1024
        ),
        cost_estimate=pl.CostEstimate(flops=flops, bytes_accessed=2 * own * columns * 3, transcendentals=0),
    )(series, band, test_matrix)


def solution(mesh):
    groups, members = mesh.devices.shape
    teams = members // TEAM
    split = Mesh(mesh.devices.reshape(groups, teams, TEAM), ("grp", "z", "q"))
    placed = (P(("z", "q"), "grp"), P(), P())
    return jax.shard_map(
        functools.partial(on_device, teams),
        mesh=split,
        in_specs=placed,
        out_specs=(P(("grp", "z", "q"), None), P("grp", None)),
        check_vma=False,
    )
```

```python
import functools

import jax
import jax.numpy as jnp
from jax import lax
from jax.experimental import pallas as pl
from jax.experimental.pallas import tpu as pltpu
from jax.sharding import Mesh, PartitionSpec as P

MESH = pl.DeviceIdType.MESH
TEAM = 4
BLOCK = 256
REACH = 86.0
TINY = 1e-30
SIDE = 16


def banded_rows(filter_taps, rows, width, lead):
    taps = filter_taps.shape[0]
    line = jnp.concatenate(
        [jnp.zeros((lead,), filter_taps.dtype), filter_taps, jnp.zeros((width + 1 - lead - taps,), filter_taps.dtype)]
    )
    return jnp.tile(line, rows)[: rows * width].reshape(rows, width)


def team_kernel(
    cut, teams, pad,
    series, band, omega, patterns, factor,
    days, filt, om, acc, got, sk, grams, tri, cross, wire, landed,
    local_sem, om_sem, send_sem, recv_sem, hsend, hrecv, ssend, srecv, gsend, grecv, msend, mrecv, rsend, rrecv,
):
    z, q = lax.axis_index("z"), lax.axis_index("q")
    own = series.shape[0]
    width = filt.shape[1]
    per = width // teams
    span = own * TEAM
    chunks = width // cut
    subs = per // cut
    up, down = lax.rem(z + 1, teams), lax.rem(z + teams - 1, teams)

    barrier = pltpu.get_barrier_semaphore()
    for d in range(1, TEAM):
        pl.semaphore_signal(barrier, inc=1, device_id={"q": lax.rem(q + d, TEAM)}, device_id_type=MESH)
    for d in range(1, teams):
        pl.semaphore_signal(barrier, inc=1, device_id={"z": lax.rem(z + d, teams)}, device_id_type=MESH)

    def source(k, member):
        start = ((k // subs) * TEAM + member) * per + (k % subs) * cut
        return series.at[:, pl.ds(pl.multiple_of(start, 128), cut)]

    def cols(k):
        return pl.ds(pl.multiple_of(k * cut, 128), cut)

    mine = pl.ds(pl.multiple_of(pad + q * own, 16), own)
    share = pl.ds(pl.multiple_of(q * own, 16), own)

    def local(k):
        return pltpu.make_async_copy(source(k, q), days.at[mine, cols(k)], local_sem.at[k])

    def omega_rows(b):
        rows = pl.ds(pl.multiple_of((b * TEAM + q) * per, 128), per)
        return pltpu.make_async_copy(omega.at[rows, :], om.at[pl.ds(b * per, per), :], om_sem.at[b])

    def give(k, d):
        peer = lax.rem(q + d, TEAM)
        return pltpu.make_async_remote_copy(
            src_ref=source(k, peer), dst_ref=days.at[mine, cols(k)],
            send_sem=send_sem.at[k, d - 1], recv_sem=recv_sem.at[k, d - 1],
            device_id={"q": peer}, device_id_type=MESH,
        )

    def take(k, d):
        origin = lax.rem(q + TEAM - d, TEAM)
        rows = pl.ds(pl.multiple_of(pad + origin * own, 16), own)
        return pltpu.make_async_remote_copy(
            src_ref=days.at[rows, cols(k)], dst_ref=days.at[rows, cols(k)],
            send_sem=send_sem.at[k, d - 1], recv_sem=recv_sem.at[k, d - 1],
            device_id={"q": origin}, device_id_type=MESH,
        )

    def halo_up(k):
        return pltpu.make_async_remote_copy(
            src_ref=days.at[pl.ds(span, pad), cols(k)], dst_ref=days.at[pl.ds(0, pad), cols(k)],
            send_sem=hsend.at[k, 0], recv_sem=hrecv.at[k, 0],
            device_id={"z": up}, device_id_type=MESH,
        )

    def halo_down(k):
        return pltpu.make_async_remote_copy(
            src_ref=days.at[pl.ds(pad, pad), cols(k)], dst_ref=days.at[pl.ds(pad + span, pad), cols(k)],
            send_sem=hsend.at[k, 1], recv_sem=hrecv.at[k, 1],
            device_id={"z": down}, device_id_type=MESH,
        )

    for b in range(teams):
        omega_rows(b).start()
    for k in range(chunks):
        local(k).start()
    pl.semaphore_wait(barrier, TEAM + teams - 2)

    def give_all(k):
        for d in (2, 1, 3):
            give(k, d).start()

    ahead = 2
    for k in range(ahead):
        give_all(k)

    @pl.when(z == 0)
    def _():
        days[:pad, :] = jnp.zeros((pad, width), days.dtype)

    @pl.when(z == teams - 1)
    def _():
        days[pad + span :, :] = jnp.zeros((pad, width), days.dtype)

    acc[...] = jnp.zeros_like(acc)
    for b in range(teams):
        omega_rows(b).wait()

    reach = band.shape[1]

    def step(k, carry):
        @pl.when(k < chunks)
        def _():
            local(k).wait()
            for d in range(1, TEAM):
                take(k, d).wait_recv()

            @pl.when(z < teams - 1)
            def _():
                halo_up(k).start()

            @pl.when(z > 0)
            def _():
                halo_down(k).start()

        @pl.when(k + ahead < chunks)
        def _():
            give_all(k + ahead)

        @pl.when(k >= 1)
        def _():
            p = k - 1

            @pl.when(z > 0)
            def _():
                halo_up(p).wait_recv()

            @pl.when(z < teams - 1)
            def _():
                halo_down(p).wait_recv()

            weights = om[pl.ds(pl.multiple_of(p * cut, 128), cut), :]
            for r in range(span // BLOCK):
                part = jnp.dot(
                    band[...], days[r * BLOCK : r * BLOCK + reach, cols(p)], preferred_element_type=jnp.float32
                ).astype(filt.dtype)
                filt[r * BLOCK : (r + 1) * BLOCK, cols(p)] = part
                acc[r * BLOCK : (r + 1) * BLOCK, :] += jnp.dot(part, weights, preferred_element_type=jnp.float32)

        return carry

    lax.fori_loop(0, chunks + 1, step, 0)

    def part_copy(d):
        peer = lax.rem(q + d, TEAM)
        rows = pl.ds(pl.multiple_of(peer * own, 16), own)
        return pltpu.make_async_remote_copy(
            src_ref=acc.at[rows, :], dst_ref=got.at[d - 1],
            send_sem=ssend.at[d - 1], recv_sem=srecv.at[d - 1],
            device_id={"q": peer}, device_id_type=MESH,
        )

    def done_copy(d):
        return pltpu.make_async_remote_copy(
            src_ref=sk.at[share, :], dst_ref=sk.at[share, :],
            send_sem=gsend.at[d - 1], recv_sem=grecv.at[d - 1],
            device_id={"q": lax.rem(q + d, TEAM)}, device_id_type=MESH,
        )

    def done_take(d):
        origin = lax.rem(q + TEAM - d, TEAM)
        rows = pl.ds(pl.multiple_of(origin * own, 16), own)
        return pltpu.make_async_remote_copy(
            src_ref=sk.at[rows, :], dst_ref=sk.at[rows, :],
            send_sem=gsend.at[d - 1], recv_sem=grecv.at[d - 1],
            device_id={"q": origin}, device_id_type=MESH,
        )

    for d in (2, 1, 3):
        part_copy(d).start()
    for d in range(1, TEAM):
        part_copy(d).wait_recv()
    total = acc[share, :] + got[0] + got[1] + got[2]
    sk[share, :] = total.astype(sk.dtype)
    for d in (2, 1, 3):
        done_copy(d).start()
    for d in range(1, TEAM):
        done_take(d).wait_recv()

    sketch = sk[...]
    turned = sketch.T
    rank = sketch.shape[1]
    grams[0] = jnp.dot(turned, sketch, preferred_element_type=jnp.float32)

    def gram_copy(d):
        return pltpu.make_async_remote_copy(
            src_ref=grams.at[0], dst_ref=grams.at[d],
            send_sem=msend.at[d - 1], recv_sem=mrecv.at[d - 1],
            device_id={"z": lax.rem(z + d, teams)}, device_id_type=MESH,
        )

    for d in range(1, teams):
        gram_copy(d).start()

    def sum_right(c):
        return pltpu.make_async_remote_copy(
            src_ref=wire.at[c], dst_ref=landed.at[c],
            send_sem=rsend.at[c], recv_sem=rrecv.at[c],
            device_id={"z": up}, device_id_type=MESH,
        )

    def sum_left(c):
        slot = jnp.where(c == down, teams, c)
        return pltpu.make_async_remote_copy(
            src_ref=wire.at[c], dst_ref=landed.at[slot],
            send_sem=rsend.at[c], recv_sem=rrecv.at[slot],
            device_id={"z": down}, device_id_type=MESH,
        )

    def arrived(slot):
        return pltpu.make_async_remote_copy(
            src_ref=landed.at[slot], dst_ref=landed.at[slot],
            send_sem=rsend.at[0], recv_sem=rrecv.at[slot],
            device_id={"z": up}, device_id_type=MESH,
        )

    order = []
    for i in range((teams + 1) // 2):
        order += [teams - 1 - i] + ([i] if i != teams - 1 - i else [])
    for c in order:
        for s in range(subs):
            k = c * subs + s
            cross[c, :, s * cut : (s + 1) * cut] = jnp.dot(
                turned, filt[:, k * cut : (k + 1) * cut], preferred_element_type=jnp.float32
            )

    def encode(c):
        for s in range(subs):
            here = slice(s * cut, (s + 1) * cut)
            value = cross[c, :, here]
            size = jnp.abs(value)
            scale = jnp.maximum(jnp.max(size, axis=0, keepdims=True), TINY).astype(wire.dtype)
            code = jnp.exp(size * (2 * REACH / scale.astype(jnp.float32)) - REACH)
            wire[c, :rank, here] = jnp.where(value < 0, -code, code).astype(wire.dtype)
            wire[c, rank:, here] = jnp.broadcast_to(scale.astype(jnp.float32), (SIDE, cut)).astype(wire.dtype)

    def absorb(c, slot):
        for s in range(subs):
            here = slice(s * cut, (s + 1) * cut)
            code = landed[slot, :rank, here].astype(jnp.float32)
            scale = landed[slot, rank:, here].astype(jnp.float32)[:1]
            size = (jnp.log(jnp.abs(code)) + REACH) * (scale * (0.5 / REACH))
            cross[c, :, here] = cross[c, :, here] + jnp.where(code < 0, -size, size)

    def pass_right(c, first):
        if not first:
            arrived(c).wait_recv()
            absorb(c, c)
        if c < teams - 1:
            sum_right(c + 1).wait_send()
        encode(c)
        sum_right(c).start()

    def pass_left(c, first):
        if not first:
            arrived(c).wait_recv()
            absorb(c, c)
        if c > 0:
            sum_left(c - 1).wait_send()
        encode(c)
        sum_left(c).start()

    def ends(i):
        if i < teams - 1:
            @pl.when(z == 0)
            def _():
                pass_right(teams - 1 - i, True)

            @pl.when(z == teams - 1)
            def _():
                pass_left(i, True)

    ends(0)
    for d in range(1, teams):
        gram_copy(d).wait_recv()
    whole = grams[0]
    for d in range(1, teams):
        whole = whole + grams[d]
    row = lax.broadcasted_iota(jnp.int32, (rank, rank), 0)
    col = lax.broadcasted_iota(jnp.int32, (rank, rank), 1)
    tri[:, :rank] = whole
    tri[:, rank:] = jnp.where(row == col, 1.0, 0.0).astype(jnp.float32)
    lane = lax.broadcasted_iota(jnp.int32, (1, rank), 1)
    eye = row == col
    below = lax.broadcasted_iota(jnp.int32, (rank, 1), 0)

    def eliminate(j, carry):
        line = tri[pl.ds(j, 1), :]
        pivot = jnp.sum(jnp.where(lane == j, line[:, :rank], 0.0), axis=1, keepdims=True)
        line = line * (1.0 / jnp.sqrt(pivot))
        mult = jnp.sum(jnp.where(eye, line[:, :rank], 0.0), axis=1, keepdims=True)
        tri[...] = tri[...] - jnp.where(below > j, mult, 0.0) * line
        tri[pl.ds(j, 1), :] = line
        return carry

    piece = rank // teams
    for i in range(teams):
        if i > 0:
            ends(i)
        lax.fori_loop(i * piece, (i + 1) * piece, eliminate, 0)
        c = teams - 1 - i
        if c > 0:
            @pl.when((z > 0) & (z < c))
            def _():
                pass_right(c, False)
        if i < teams - 1:
            @pl.when((z < teams - 1) & (z > i))
            def _():
                pass_left(i, False)

    upper = jnp.where(row <= col, tri[:, :rank], 0.0)
    factor[...] = upper * float(span * teams) ** (-0.5)
    inverse = jnp.where(row >= col, tri[:, rank:], 0.0)

    @pl.when(z > 0)
    def _():
        arrived(z).wait_recv()
        absorb(z, z)

    @pl.when(z < teams - 1)
    def _():
        arrived(teams).wait_recv()
        absorb(z, teams)

    for s in range(subs):
        solved = jnp.dot(
            inverse, cross[z, :, s * cut : (s + 1) * cut],
            preferred_element_type=jnp.float32, precision=lax.Precision.HIGHEST,
        )
        patterns[s * cut : (s + 1) * cut, :] = solved.T

    def drain(k, carry):
        for d in range(1, TEAM):
            give(k, d).wait_send()

        @pl.when(z < teams - 1)
        def _():
            halo_up(k).wait_send()

        @pl.when(z > 0)
        def _():
            halo_down(k).wait_send()

        return carry

    lax.fori_loop(0, chunks, drain, 0)
    for d in range(1, TEAM):
        part_copy(d).wait_send()
        done_copy(d).wait_send()
    for d in range(1, teams):
        gram_copy(d).wait_send()

    @pl.when(z < teams - 1)
    def _():
        sum_right(z + 1).wait_send()

    @pl.when(z > 0)
    def _():
        sum_left(z - 1).wait_send()


def on_device(teams, series, filter_taps, test_matrix):
    own, columns = series.shape
    rank = test_matrix.shape[1]
    half_width = (filter_taps.shape[0] - 1) // 2
    pad = -(-half_width // 16) * 16
    span = own * TEAM
    width = columns // TEAM
    per = width // teams
    cut = per // 2 if per % 256 == 0 and per > 512 else per
    chunks = width // cut
    band = banded_rows(filter_taps, BLOCK, BLOCK + 2 * pad, pad - half_width)
    vmem = pl.BlockSpec(memory_space=pltpu.VMEM)
    hbm = pl.BlockSpec(memory_space=pl.ANY)
    dma = pltpu.SemaphoreType.DMA
    flops = 2 * span * width * (BLOCK + 2 * pad + 2 * rank)
    return pl.pallas_call(
        functools.partial(team_kernel, cut, teams, pad),
        out_shape=(
            jax.ShapeDtypeStruct((per, rank), jnp.float32),
            jax.ShapeDtypeStruct((rank, rank), jnp.float32),
        ),
        in_specs=[hbm, vmem, hbm],
        out_specs=(vmem, vmem),
        scratch_shapes=[
            pltpu.VMEM((span + 2 * pad, width), jnp.bfloat16),
            pltpu.VMEM((span, width), jnp.bfloat16),
            pltpu.VMEM((width, rank), jnp.bfloat16),
            pltpu.VMEM((span, rank), jnp.float32),
            pltpu.VMEM((TEAM - 1, own, rank), jnp.float32),
            pltpu.VMEM((span, rank), jnp.bfloat16),
            pltpu.VMEM((teams, rank, rank), jnp.float32),
            pltpu.VMEM((rank, 2 * rank), jnp.float32),
            pltpu.VMEM((teams, rank, per), jnp.float32),
            pltpu.VMEM((teams, rank + SIDE, per), jnp.bfloat16),
            pltpu.VMEM((teams + 1, rank + SIDE, per), jnp.bfloat16),
            dma((chunks,)),
            dma((teams,)),
            dma((chunks, TEAM - 1)),
            dma((chunks, TEAM - 1)),
            dma((chunks, 2)),
            dma((chunks, 2)),
            dma((TEAM - 1,)),
            dma((TEAM - 1,)),
            dma((TEAM - 1,)),
            dma((TEAM - 1,)),
            dma((teams - 1,)),
            dma((teams - 1,)),
            dma((teams,)),
            dma((teams + 1,)),
        ],
        compiler_params=pltpu.CompilerParams(
            collective_id=0, has_side_effects=True, vmem_limit_bytes=56 * 1024 * 1024
        ),
        cost_estimate=pl.CostEstimate(flops=flops, bytes_accessed=2 * own * columns * 3, transcendentals=0),
    )(series, band, test_matrix)


def solution(mesh):
    groups, members = mesh.devices.shape
    teams = members // TEAM
    split = Mesh(mesh.devices.reshape(groups, teams, TEAM), ("grp", "z", "q"))
    placed = (P(("z", "q"), "grp"), P(), P())
    return jax.shard_map(
        functools.partial(on_device, teams),
        mesh=split,
        in_specs=placed,
        out_specs=(P(("grp", "z", "q"), None), P("grp", None)),
        check_vma=False,
    )
```
